1024 devices in a mesh: row: 32 (over x, z_hi, y), col: 16 (over z_lo), layer: 2 (over core).
Axes of the slice: x: 4, y: 4, z: 32 (z_hi: 2, z_lo: 16; z = z_hi * 16 + z_lo), core: 2. Of those that a mesh axis runs over, the one named last changes fastest.
Arguments:
- left_panels: bfloat16 [32, 16, 2, 32, 128, 128], P('row', 'col', 'layer'), may hold values from -6 to 6
- right_panels: bfloat16 [32, 16, 2, 32, 128, 128], P('row', 'col', 'layer'), may hold values from -0.09375 to 0.09375
- left_picks: int32 [32, 16, 2, 4, 16, 4], P('row', 'col', 'layer'), may hold values from 0 to 31
- right_picks: int32 [32, 16, 2, 4, 16, 4], P('row', 'col', 'layer'), may hold values from 0 to 31
- live_count: int32 [32, 16, 2, 4, 16], P('row', 'col', 'layer'), may hold values from 0 to 4, as said below
Outputs:
- product_blocks: float32 [32, 16, 16, 128, 128], P('row', 'col', 'layer')
The draws below stay inside these ranges and needn't reach their ends.
Inputs may be any that keep to these rules, and one draw needn't show every extreme that they name: live_count[r, c, l, s, j] counts the leading pairs q < live_count of product block j that take part at step s; the value 4 occurs in every draw.
All inputs are finite; a program needn't handle non-finite values.
Results may differ from the reference program's by a relative error of at most 0.0003.
Values may be sent and summed in bfloat16 or wider, within the bound.
A program may use at most 32 MiB of HBM per device.

```python
import jax
import jax.numpy as jnp
from jax import lax

BS = 128
CAP = 32
CB = 16
Q = 4
STEPS = 4
N_ROW = 32
N_COL = 16
N_LAYER = 2


def draw_live_count(key, part):
    key = jax.random.fold_in(key, 7)
    first_key, second_key, third_key = jax.random.split(key, 3)
    ceiling = jax.random.randint(first_key, (N_ROW, N_COL, N_LAYER, 1, 1), 1, Q + 1)
    floor_count = ceiling // 2
    raw_bits = jax.random.randint(second_key, (N_ROW, N_COL, N_LAYER, STEPS, CB), 0, 1 << 20)
    counts = floor_count + raw_bits % (ceiling - floor_count + 1)
    entries = N_ROW * N_COL * N_LAYER * STEPS * CB
    position = jax.random.randint(third_key, (), 0, entries)
    flat_counts = jnp.where(jnp.arange(entries, dtype=jnp.int32) == position, Q, counts.reshape(-1))
    return flat_counts.reshape(counts.shape).astype(jnp.int32)


def plant(values, key, least, largest):
    longest = values.shape.index(max(values.shape))
    spots = []
    for shift in (0, 1):
        where = [jax.random.randint(jax.random.fold_in(key, axis), (), 0, length) for axis, length in enumerate(values.shape)]
        where[longest] = (where[longest] + shift) % values.shape[longest]
        spots.append(tuple(where))
    return values.at[spots[0]].set(least).at[spots[1]].set(largest)


def steps_of(rng, shape, pieces, least, largest):
    def one(dim, parts):
        heights = jax.random.uniform(jax.random.fold_in(jax.random.fold_in(rng, 6), dim), (parts,), jnp.float32, least / len(pieces), largest / len(pieces))
        return jnp.repeat(jnp.exp(heights), shape[dim] // parts).reshape((-1,) + (1,) * (len(shape) - dim - 1))

    factor_of = one(*pieces[0])
    for cut in pieces[1:]:
        factor_of = factor_of * one(*cut)
    return factor_of


def bell_draw(own_key, dims, spread, reach, shards=(), held_as=jnp.bfloat16):
    array = jax.random.normal(own_key, dims, jnp.float32) * spread
    if len(shards) > 0:
        array = steps_of(own_key, dims, shards, -0.22, 0.18) * array
    return jnp.clip(array, min=-reach, max=reach).astype(held_as)


def setup_inputs(seed: int = 0) -> dict:
    seeds = jax.random.split(jax.random.key(seed), 6)
    left_panels = bell_draw(seeds[0], (N_ROW, N_COL, N_LAYER, CAP, BS, BS), 1.0, 6.0, ((0, 32), (1, 16), (2, 2)))
    right_panels = bell_draw(seeds[1], (N_ROW, N_COL, N_LAYER, CAP, BS, BS), (BS * Q * STEPS * N_LAYER) ** -0.5, 0.09375, ((0, 32), (1, 16), (2, 2)))
    left_picks = plant(jax.random.randint(seeds[2], (N_ROW, N_COL, N_LAYER, STEPS, CB, Q), 0, CAP), jax.random.fold_in(seeds[2], 1), 0, CAP - 1).astype(jnp.int32)
    right_picks = plant(jax.random.randint(seeds[3], (N_ROW, N_COL, N_LAYER, STEPS, CB, Q), 0, CAP), jax.random.fold_in(seeds[3], 1), 0, CAP - 1).astype(jnp.int32)
    live_count = draw_live_count(jax.random.fold_in(seeds[5], 71), 0)
    return dict(left_panels=left_panels, right_panels=right_panels, left_picks=left_picks, right_picks=right_picks, live_count=live_count)


def select_blocks(panel, picks, active):
    padded = jnp.concatenate([panel, jnp.zeros((1,) + panel.shape[1:], panel.dtype)], axis=0)
    chosen = jnp.where(active, picks, jnp.int32(panel.shape[0])).astype(jnp.int32)
    return padded[chosen]


def block_step(left_panel, right_panel, left_list, right_list, counts):
    active = jnp.arange(left_list.shape[-1], dtype=jnp.int32)[None, :] < counts[:, None]
    left_sel = select_blocks(left_panel, left_list, active).astype(jnp.float32)
    right_sel = select_blocks(right_panel, right_list, active).astype(jnp.float32)
    return jnp.einsum("cqik,cqkj->cij", left_sel, right_sel)


def reference(left_panels, right_panels, left_picks, right_picks, live_count):
    def grid_position(flat_index):
        row_index = flat_index // N_COL
        col_index = flat_index % N_COL
        totals = jnp.zeros((CB, BS, BS), jnp.float32)
        for layer_index in range(N_LAYER):
            for step in range(STEPS):
                left_panel = left_panels[row_index, (col_index + step) % N_COL, layer_index]
                right_panel = right_panels[(row_index + step) % N_ROW, col_index, layer_index]
                totals = totals + block_step(left_panel, right_panel,
                                             left_picks[row_index, col_index, layer_index, step],
                                             right_picks[row_index, col_index, layer_index, step],
                                             live_count[row_index, col_index, layer_index, step])
        return totals

    summed = lax.map(grid_position, jnp.arange(N_ROW * N_COL, dtype=jnp.int32))
    return summed.reshape(N_ROW, N_COL, CB, BS, BS)
```

```python
import functools

import jax
import jax.numpy as jnp
from jax import lax
from jax.experimental import pallas as pl
from jax.experimental.pallas import tpu as pltpu
from jax.sharding import PartitionSpec as P

MESH = pl.DeviceIdType.MESH

STEPS = 4
NY = 4
BS = 128
CAP = 32
CB = 16
Q = 4
CHUNKS = 3
LANE = 4
LEFT = 2


def kernel(
    nx, nc,
    lp_ref, rp_ref, live_ref, left_hbm, right_hbm, out_ref,
    lown, rown, lbuf, rbuf, lane, totals, partner,
    own_sem, lane_send, lane_recv, left_send, left_recv, wrap_send,
    seed_send, seed_recv, near_send, right_recv, spread_send, sum_send, sum_recv,
):
    hops = nc
    items = hops * CHUNKS
    lag = CAP // LEFT
    row = lax.axis_index("row")
    c = lax.axis_index("col")
    l = lax.axis_index("layer")
    x = row // (2 * NY)
    h = (row // NY) % 2
    y = row % NY

    def at(px, ph, py, pc, pll):
        return (px * (2 * NY) + ph * NY + py, pc, pll)

    def ring(px):
        return lax.rem(px + nx, nx)

    first, last = c == 0, c == nc - 1
    up_c = jnp.where(last, 0, c + 1)
    down_c = jnp.where(first, nc - 1, c - 1)
    up_h = jnp.where(last, 1 - h, h)
    down_h = jnp.where(first, 1 - h, h)
    up_next = at(ring(x - jnp.where(last & (h == 0), 1, 0)), up_h, y, up_c, l)
    up_prev = at(ring(x + jnp.where(first & (h == 1), 1, 0)), down_h, y, down_c, l)
    down_next = at(ring(x - jnp.where(first & (h == 0), 1, 0)), down_h, y, down_c, l)
    down_prev = at(ring(x + jnp.where(last & (h == 1), 1, 0)), up_h, y, up_c, l)
    nexts = (up_next, down_next)

    def in_group(py):
        return at(x, h, py, c, l)

    def on_col(pc):
        return at(x, h, y, pc, l)

    sibling = at(x, h, y, c, 1 - l)

    own_left = pltpu.make_async_copy(left_hbm, lown.at[pl.ds(0, CAP)], own_sem.at[0])
    own_right = pltpu.make_async_copy(right_hbm, rown, own_sem.at[1])
    own_left.start()
    own_right.start()

    def own_lane(d):
        return pltpu.make_async_copy(
            right_hbm.at[pl.ds(d * CHUNKS * LANE, CHUNKS * LANE)],
            lane.at[d, pl.ds(0, CHUNKS * LANE)],
            own_sem.at[2 + d],
        )

    @pl.when(y < NY - 1)
    def _():
        own_lane(0).start()
        own_lane(1).start()

    lown[CAP] = jnp.zeros((BS, BS), lown.dtype)
    lbuf[(STEPS - 1) * CAP] = jnp.zeros((BS, BS), lbuf.dtype)

    barrier = pltpu.get_barrier_semaphore()
    for who in (up_prev, down_prev, sibling):
        pl.semaphore_signal(barrier, inc=1, device_id=who, device_id_type=MESH)
    for k in range(1, NY):
        pl.semaphore_signal(
            barrier, inc=1, device_id=in_group(lax.rem(y + k, NY)), device_id_type=MESH
        )

    @pl.when(c < nc - 1)
    def _():
        pl.semaphore_signal(barrier, inc=1, device_id=on_col(c + 1), device_id_type=MESH)

    @pl.when(last)
    def _():
        for k in range(STEPS - 1):
            pl.semaphore_signal(barrier, inc=1, device_id=on_col(k), device_id_type=MESH)

    greeted = 3 + (NY - 1) + jnp.where(c > 0, 1, 0) + jnp.where(c < STEPS - 1, 1, 0)
    pl.semaphore_wait(barrier, greeted)

    spare = 2 * CHUNKS * LANE

    def seed(d, who):
        return pltpu.make_async_remote_copy(
            src_ref=right_hbm.at[pl.ds(spare + d * LANE, LANE)],
            dst_ref=lane.at[d, pl.ds(who * LANE, LANE)],
            send_sem=seed_send.at[d],
            recv_sem=seed_recv.at[d, who],
            device_id=in_group(NY - 1),
            device_id_type=MESH,
        )

    @pl.when(y < NY - 1)
    def _():
        seed(0, y).start()
        seed(1, y).start()
        own_lane(0).wait()
        own_lane(1).wait()

    own_left.wait()
    own_right.wait()

    def lane_copy(d, it):
        return pltpu.make_async_remote_copy(
            src_ref=lane.at[d, pl.ds(it * LANE, LANE)],
            dst_ref=lane.at[d, pl.ds((it + CHUNKS) * LANE, LANE)],
            send_sem=lane_send.at[d, it],
            recv_sem=lane_recv.at[d, it],
            device_id=nexts[d],
            device_id_type=MESH,
        )

    def left_copy(it, src=None):
        if src is None:
            src = lbuf.at[pl.ds(it * LEFT, LEFT)]
        return pltpu.make_async_remote_copy(
            src_ref=src,
            dst_ref=lbuf.at[pl.ds(it * LEFT, LEFT)],
            send_sem=left_send.at[it],
            recv_sem=left_recv.at[it],
            device_id=on_col(jnp.maximum(c - 1, 0)),
            device_id_type=MESH,
        )

    def wrap_copy(it):
        return pltpu.make_async_remote_copy(
            src_ref=lown.at[pl.ds(lax.rem(it, lag) * LEFT, LEFT)],
            dst_ref=lbuf.at[pl.ds(it * LEFT, LEFT)],
            send_sem=wrap_send.at[lax.rem(it, lag)],
            recv_sem=left_recv.at[it],
            device_id=on_col(nc - 1),
            device_id_type=MESH,
        )

    near = 4
    near_copies = CAP // near

    def near_copy(s, k):
        return pltpu.make_async_remote_copy(
            src_ref=rown.at[pl.ds(k * near, near)],
            dst_ref=rbuf.at[pl.ds((s - 1) * CAP + k * near, near)],
            send_sem=near_send.at[s - 1, k],
            recv_sem=right_recv.at[s - 1],
            device_id=in_group(jnp.maximum(y - s, 0)),
            device_id_type=MESH,
        )

    def pair_sum(j, s):
        lefts, rights = [], []
        for q in range(Q):
            index = (s * CB + j) * Q + q
            used = q < live_ref[s * CB + j]
            if s == 0:
                lefts.append(lown[jnp.where(used, lp_ref[index], CAP)])
                rights.append(rown[rp_ref[index]])
            else:
                base = (s - 1) * CAP
                lefts.append(lbuf[jnp.where(used, base + lp_ref[index], (STEPS - 1) * CAP)])
                rights.append(rbuf[base + rp_ref[index]])
        return jnp.dot(
            jnp.concatenate(lefts, axis=1),
            jnp.concatenate(rights, axis=0),
            preferred_element_type=jnp.float32,
        )

    def step(it, _):
        @pl.when(it >= CHUNKS)
        def _():
            for d in range(2):
                lane_copy(d, it - CHUNKS).wait_recv()

        @pl.when((it < CHUNKS) & (y == NY - 1))
        def _():
            for d in range(2):
                seed(d, it).wait_recv()

        for d in range(2):
            lane_copy(d, it).start()

        @pl.when(it >= lag)
        def _():
            left_copy(it - lag).wait_recv()

        @pl.when((c > 0) & (it < lag))
        def _():
            left_copy(it, lown.at[pl.ds(it * LEFT, LEFT)]).start()

        @pl.when((c > 0) & (it >= lag))
        def _():
            left_copy(it, lbuf.at[pl.ds((it - lag) * LEFT, LEFT)]).start()

        @pl.when(it // lag == c)
        def _():
            wrap_copy(it).start()

        @pl.when((it >= CHUNKS) & (it < CHUNKS + near_copies))
        def _():
            for s in range(1, STEPS):

                @pl.when(y >= s)
                def _():
                    near_copy(s, it - CHUNKS).start()

        @pl.when(lax.rem(it, CHUNKS) == 2)
        def _():
            j = it // CHUNKS
            totals[j] = pair_sum(j, 0)

        return 0

    lax.fori_loop(0, items, step, 0)

    def spread(d, ch, to):
        src = jnp.where(y < NY - 1, y, ch)
        block = jnp.where(y < NY - 1, (d * CHUNKS + ch) * LANE, spare + d * LANE)
        start = (NY + src - to - 1) * CAP + block
        return src, start

    def spread_copy(d, ch, to):
        src, start = spread(d, ch, to)
        return pltpu.make_async_remote_copy(
            src_ref=lane.at[d, pl.ds((items + ch) * LANE, LANE)],
            dst_ref=rbuf.at[pl.ds(start, LANE)],
            send_sem=spread_send.at[d, ch, to - 1],
            recv_sem=right_recv.at[NY + src - to - 1],
            device_id=in_group(to),
            device_id_type=MESH,
        )

    def spread_here(d, ch):
        src, start = spread(d, ch, NY - 1)
        return pltpu.make_async_copy(
            lane.at[d, pl.ds((items + ch) * LANE, LANE)],
            rbuf.at[pl.ds(start, LANE)],
            right_recv.at[src],
        )

    for ch in range(CHUNKS):
        for d in range(2):
            lane_copy(d, items - CHUNKS + ch).wait_recv()
            for to in range(1, NY):
                src, _ = spread(d, ch, to)

                @pl.when((to > src) & (to != y))
                def _():
                    spread_copy(d, ch, to).start()

            @pl.when(y == NY - 1)
            def _():
                spread_here(d, ch).start()

    lax.fori_loop(items - lag, items, lambda it, _: (left_copy(it).wait_recv(), 0)[1], 0)
    for s in range(1, STEPS):
        panel = rbuf.at[pl.ds((s - 1) * CAP, CAP)]
        pltpu.make_async_copy(panel, panel, right_recv.at[s - 1]).wait()

    half = CB // 2

    def rest(j):
        total = totals[j]
        for s in range(1, STEPS):
            total = total + pair_sum(j, s)
        return total

    def sum_copy(i):
        return pltpu.make_async_remote_copy(
            src_ref=totals.at[(1 - l) * half + i],
            dst_ref=partner.at[i],
            send_sem=sum_send.at[i],
            recv_sem=sum_recv.at[i],
            device_id=sibling,
            device_id_type=MESH,
        )

    def theirs(i, _):
        j = (1 - l) * half + i
        totals[j] = rest(j)
        sum_copy(i).start()
        return 0

    def ours(i, _):
        out_ref[i] = rest(l * half + i)
        return 0

    lax.fori_loop(0, half, theirs, 0)
    lax.fori_loop(0, half, ours, 0)

    def lanes_gone(it, _):
        for d in range(2):
            lane_copy(d, it).wait_send()

        @pl.when(c > 0)
        def _():
            left_copy(it).wait_send()

        @pl.when(it // lag == c)
        def _():
            wrap_copy(it).wait_send()

        return 0

    lax.fori_loop(0, items, lanes_gone, 0)

    @pl.when(y < NY - 1)
    def _():
        seed(0, y).wait_send()
        seed(1, y).wait_send()

    for s in range(1, STEPS):

        @pl.when(y >= s)
        def _():
            lax.fori_loop(0, near_copies, lambda k, _: (near_copy(s, k).wait_send(), 0)[1], 0)

    for ch in range(CHUNKS):
        for d in range(2):
            for to in range(1, NY):
                src, _ = spread(d, ch, to)

                @pl.when((to > src) & (to != y))
                def _():
                    spread_copy(d, ch, to).wait_send()

    def finish(i, _):
        sum_copy(i).wait_recv()
        out_ref[i] = out_ref[i] + partner[i]
        sum_copy(i).wait_send()
        return 0

    lax.fori_loop(0, half, finish, 0)


def solution(mesh):
    nx = mesh.shape["row"] // (2 * NY)
    nc = mesh.shape["col"]
    items = nc * CHUNKS
    dma = pltpu.SemaphoreType.DMA

    def local(left_panels, right_panels, left_picks, right_picks, live_count):
        summed = pl.pallas_call(
            functools.partial(kernel, nx, nc),
            out_shape=jax.ShapeDtypeStruct((CB // 2, BS, BS), jnp.float32),
            in_specs=[pl.BlockSpec(memory_space=pltpu.SMEM)] * 3
            + [pl.BlockSpec(memory_space=pl.ANY)] * 2,
            out_specs=pl.BlockSpec(memory_space=pltpu.VMEM),
            scratch_shapes=[
                pltpu.VMEM((CAP + 1, BS, BS), jnp.bfloat16),
                pltpu.VMEM((CAP, BS, BS), jnp.bfloat16),
                pltpu.VMEM(((STEPS - 1) * CAP + 1, BS, BS), jnp.bfloat16),
                pltpu.VMEM(((STEPS - 1) * CAP, BS, BS), jnp.bfloat16),
                pltpu.VMEM((2, (items + CHUNKS) * LANE, BS, BS), jnp.bfloat16),
                pltpu.VMEM((CB, BS, BS), jnp.float32),
                pltpu.VMEM((CB // 2, BS, BS), jnp.float32),
                dma((4,)),
                dma((2, items)),
                dma((2, items)),
                dma((items,)),
                dma((items,)),
                dma((CAP // LEFT,)),
                dma((2,)),
                dma((2, CHUNKS)),
                dma((STEPS - 1, CAP // 4)),
                dma((STEPS - 1,)),
                dma((2, CHUNKS, NY - 1)),
                dma((CB // 2,)),
                dma((CB // 2,)),
            ],
            compiler_params=pltpu.CompilerParams(
                collective_id=0, has_side_effects=True, vmem_limit_bytes=48 * 2**20
            ),
            name="cannon_window",
        )(
            left_picks.reshape(-1),
            right_picks.reshape(-1),
            live_count.reshape(-1),
            left_panels[0, 0, 0],
            right_panels[0, 0, 0],
        )
        return summed[None, None]

    placed = (
        P("row", "col", "layer", None, None, None),
        P("row", "col", "layer", None, None, None),
        P("row", "col", "layer", None, None, None),
        P("row", "col", "layer", None, None, None),
        P("row", "col", "layer", None, None),
    )
    return jax.shard_map(
        local,
        mesh=mesh,
        in_specs=placed,
        out_specs=P("row", "col", "layer", None, None),
        check_vma=False,
    )
```

```python
import functools

import jax
import jax.numpy as jnp
from jax import lax
from jax.experimental import pallas as pl
from jax.experimental.pallas import tpu as pltpu
from jax.sharding import PartitionSpec as P

MESH = pl.DeviceIdType.MESH

STEPS = 4
NY = 4
BS = 128
CAP = 32
CB = 16
Q = 4
CHUNKS = 3
LANE = 4
LEFT = 2
LEAD = 8


def kernel(
    nx, nc,
    lp_ref, rp_ref, live_ref, left_hbm, right_hbm, out_ref,
    left0, left1, left2, left3, right0, right1, right2, right3, lane, totals, partner,
    own_sem, lane_send, lane_recv, left_send, left_recv, wrap_send,
    seed_send, seed_recv, near_send, right_recv, spread_send, sum_send, sum_recv,
):
    hops = nc
    items = hops * CHUNKS
    lag = CAP // LEFT
    lefts_at, rights_at = (left0, left1, left2, left3), (right0, right1, right2, right3)
    row = lax.axis_index("row")
    c = lax.axis_index("col")
    l = lax.axis_index("layer")
    x = row // (2 * NY)
    h = (row // NY) % 2
    y = row % NY

    def at(px, ph, py, pc, pll):
        return (px * (2 * NY) + ph * NY + py, pc, pll)

    def ring(px):
        return lax.rem(px + nx, nx)

    first, last = c == 0, c == nc - 1
    up_c = jnp.where(last, 0, c + 1)
    down_c = jnp.where(first, nc - 1, c - 1)
    up_h = jnp.where(last, 1 - h, h)
    down_h = jnp.where(first, 1 - h, h)
    up_next = at(ring(x - jnp.where(last & (h == 0), 1, 0)), up_h, y, up_c, l)
    up_prev = at(ring(x + jnp.where(first & (h == 1), 1, 0)), down_h, y, down_c, l)
    down_next = at(ring(x - jnp.where(first & (h == 0), 1, 0)), down_h, y, down_c, l)
    down_prev = at(ring(x + jnp.where(last & (h == 1), 1, 0)), up_h, y, up_c, l)
    nexts = (up_next, down_next)

    def in_group(py):
        return at(x, h, py, c, l)

    def on_col(pc):
        return at(x, h, y, pc, l)

    sibling = at(x, h, y, c, 1 - l)

    own_left = pltpu.make_async_copy(left_hbm, left0.at[pl.ds(0, CAP)], own_sem.at[0])
    own_right = pltpu.make_async_copy(right_hbm, right0, own_sem.at[1])
    own_left.start()
    own_right.start()

    def own_lane(d):
        return pltpu.make_async_copy(
            right_hbm.at[pl.ds(d * CHUNKS * LANE, CHUNKS * LANE)],
            lane.at[d, pl.ds(0, CHUNKS * LANE)],
            own_sem.at[2 + d],
        )

    @pl.when(y < NY - 1)
    def _():
        own_lane(0).start()
        own_lane(1).start()

    for panel in lefts_at:
        panel[CAP] = jnp.zeros((BS, BS), panel.dtype)

    barrier = pltpu.get_barrier_semaphore()
    for who in (up_prev, down_prev, sibling):
        pl.semaphore_signal(barrier, inc=1, device_id=who, device_id_type=MESH)
    for k in range(1, NY):
        pl.semaphore_signal(
            barrier, inc=1, device_id=in_group(lax.rem(y + k, NY)), device_id_type=MESH
        )

    @pl.when(c < nc - 1)
    def _():
        pl.semaphore_signal(barrier, inc=1, device_id=on_col(c + 1), device_id_type=MESH)

    @pl.when(last)
    def _():
        for k in range(STEPS - 1):
            pl.semaphore_signal(barrier, inc=1, device_id=on_col(k), device_id_type=MESH)

    greeted = 3 + (NY - 1) + jnp.where(c > 0, 1, 0) + jnp.where(c < STEPS - 1, 1, 0)
    pl.semaphore_wait(barrier, greeted)

    spare = 2 * CHUNKS * LANE

    def seed(d, who):
        return pltpu.make_async_remote_copy(
            src_ref=right_hbm.at[pl.ds(spare + d * LANE, LANE)],
            dst_ref=lane.at[d, pl.ds(who * LANE, LANE)],
            send_sem=seed_send.at[d],
            recv_sem=seed_recv.at[d, who],
            device_id=in_group(NY - 1),
            device_id_type=MESH,
        )

    @pl.when(y < NY - 1)
    def _():
        seed(0, y).start()
        seed(1, y).start()
        own_lane(0).wait()
        own_lane(1).wait()

    own_left.wait()
    own_right.wait()

    def lane_copy(d, it):
        return pltpu.make_async_remote_copy(
            src_ref=lane.at[d, pl.ds(it * LANE, LANE)],
            dst_ref=lane.at[d, pl.ds((it + CHUNKS) * LANE, LANE)],
            send_sem=lane_send.at[d, it],
            recv_sem=lane_recv.at[d, it],
            device_id=nexts[d],
            device_id_type=MESH,
        )

    def left_copy(n, step=1):
        block = pl.ds(lax.rem(n, lag) * LEFT, LEFT)
        return pltpu.make_async_remote_copy(
            src_ref=lefts_at[step - 1].at[block],
            dst_ref=lefts_at[step].at[block],
            send_sem=left_send.at[n],
            recv_sem=left_recv.at[n],
            device_id=on_col(jnp.maximum(c - 1, 0)),
            device_id_type=MESH,
        )

    def wrap_copy(n, step=1):
        block = pl.ds(lax.rem(n, lag) * LEFT, LEFT)
        return pltpu.make_async_remote_copy(
            src_ref=left0.at[block],
            dst_ref=lefts_at[step].at[block],
            send_sem=wrap_send.at[lax.rem(n, lag)],
            recv_sem=left_recv.at[n],
            device_id=on_col(nc - 1),
            device_id_type=MESH,
        )

    def left_move(n):
        @pl.when(n >= lag)
        def _():
            left_copy(n - lag).wait_recv()

        for step in range(1, STEPS):

            @pl.when(n // lag == step - 1)
            def _():
                @pl.when(c > 0)
                def _():
                    left_copy(n, step).start()

                @pl.when(c == step - 1)
                def _():
                    wrap_copy(n, step).start()

    def left_run(start, stop):
        lax.fori_loop(start, stop, lambda n, _: (left_move(n), 0)[1], 0)

    near = 4
    near_copies = CAP // near

    def near_copy(s, k):
        return pltpu.make_async_remote_copy(
            src_ref=right0.at[pl.ds(k * near, near)],
            dst_ref=rights_at[s].at[pl.ds(k * near, near)],
            send_sem=near_send.at[s - 1, k],
            recv_sem=right_recv.at[s - 1],
            device_id=in_group(jnp.maximum(y - s, 0)),
            device_id_type=MESH,
        )

    def pair_sum(j, s):
        lefts, rights = [], []
        for q in range(Q):
            index = (s * CB + j) * Q + q
            used = q < live_ref[s * CB + j]
            lefts.append(lefts_at[s][jnp.where(used, lp_ref[index], CAP)])
            rights.append(rights_at[s][rp_ref[index]])
        return jnp.dot(
            jnp.concatenate(lefts, axis=1),
            jnp.concatenate(rights, axis=0),
            preferred_element_type=jnp.float32,
        )

    def step(it, _):
        for d in range(2):

            @pl.when(it >= CHUNKS)
            def _():
                lane_copy(d, it - CHUNKS).wait_recv()

            @pl.when((it < CHUNKS) & (y == NY - 1))
            def _():
                seed(d, it).wait_recv()

            lane_copy(d, it).start()

        @pl.when(lax.rem(it, 2) == 1)
        def _():
            left_move(lead + it // 2)

        @pl.when((it >= CHUNKS) & (it < CHUNKS + near_copies))
        def _():
            for s in range(1, STEPS):

                @pl.when(y >= s)
                def _():
                    near_copy(s, it - CHUNKS).start()

        @pl.when(lax.rem(it, CHUNKS) == 2)
        def _():
            j = it // CHUNKS
            totals[j] = pair_sum(j, 0)

        return 0

    lead = jnp.where(y == NY - 1, LEAD, 0)
    left_run(0, lead)
    lax.fori_loop(0, items, step, 0)

    def arrived(ch):
        return jnp.where(y < NY - 1, y, ch)

    def spread_copy(d, ch, s, to):
        block = jnp.where(y < NY - 1, (d * CHUNKS + ch) * LANE, spare + d * LANE)
        return pltpu.make_async_remote_copy(
            src_ref=lane.at[d, pl.ds((items + ch) * LANE, LANE)],
            dst_ref=rights_at[s].at[pl.ds(block, LANE)],
            send_sem=spread_send.at[d, ch, to - 1],
            recv_sem=right_recv.at[s - 1],
            device_id=in_group(to),
            device_id_type=MESH,
        )

    def spread_here(d, ch):
        return pltpu.make_async_copy(
            lane.at[d, pl.ds((items + ch) * LANE, LANE)],
            rights_at[ch + 1].at[pl.ds(spare + d * LANE, LANE)],
            right_recv.at[ch],
        )

    def each_spread(d, ch, act):
        for to in range(1, NY):
            for src in range(to):

                @pl.when((arrived(ch) == src) & (to != y))
                def _():
                    act(spread_copy(d, ch, NY + src - to, to))

    begun = lead + items // 2
    left_run(begun, begun + 4)
    for ch in range(CHUNKS):
        for d in range(2):
            lane_copy(d, items - CHUNKS + ch).wait_recv()
            each_spread(d, ch, lambda copy: copy.start())

            @pl.when(y == NY - 1)
            def _():
                spread_here(d, ch).start()

        left_run(begun + 4 + 2 * ch, begun + 6 + 2 * ch)
    left_run(begun + 10, items)

    def right_wait(s):
        pltpu.make_async_copy(rights_at[s], rights_at[s], right_recv.at[s - 1]).wait()

    right_wait(1)
    right_wait(2)

    def middle(j, _):
        totals[j] = totals[j] + (pair_sum(j, 1) + pair_sum(j, 2))
        return 0

    lax.fori_loop(0, CB, middle, 0)
    right_wait(3)
    lax.fori_loop(items - lag, items, lambda n, _: (left_copy(n).wait_recv(), 0)[1], 0)

    half = CB // 2

    def rest(j):
        return totals[j] + pair_sum(j, 3)

    def sum_copy(i):
        return pltpu.make_async_remote_copy(
            src_ref=totals.at[(1 - l) * half + i],
            dst_ref=partner.at[i],
            send_sem=sum_send.at[i],
            recv_sem=sum_recv.at[i],
            device_id=sibling,
            device_id_type=MESH,
        )

    def theirs(i, _):
        j = (1 - l) * half + i
        totals[j] = rest(j)
        sum_copy(i).start()
        return 0

    def ours(i, _):
        out_ref[i] = rest(l * half + i)
        return 0

    lax.fori_loop(0, half, theirs, 0)
    lax.fori_loop(0, half, ours, 0)

    def lanes_gone(it, _):
        for d in range(2):
            lane_copy(d, it).wait_send()

        @pl.when(c > 0)
        def _():
            left_copy(it).wait_send()

        @pl.when(it // lag == c)
        def _():
            wrap_copy(it).wait_send()

        return 0

    lax.fori_loop(0, items, lanes_gone, 0)

    @pl.when(y < NY - 1)
    def _():
        seed(0, y).wait_send()
        seed(1, y).wait_send()

    for s in range(1, STEPS):

        @pl.when(y >= s)
        def _():
            lax.fori_loop(0, near_copies, lambda k, _: (near_copy(s, k).wait_send(), 0)[1], 0)

    for ch in range(CHUNKS):
        for d in range(2):
            each_spread(d, ch, lambda copy: copy.wait_send())

    def finish(i, _):
        sum_copy(i).wait_recv()
        out_ref[i] = out_ref[i] + partner[i]
        sum_copy(i).wait_send()
        return 0

    lax.fori_loop(0, half, finish, 0)


def solution(mesh):
    nx = mesh.shape["row"] // (2 * NY)
    nc = mesh.shape["col"]
    items = nc * CHUNKS
    dma = pltpu.SemaphoreType.DMA

    def local(left_panels, right_panels, left_picks, right_picks, live_count):
        summed = pl.pallas_call(
            functools.partial(kernel, nx, nc),
            out_shape=jax.ShapeDtypeStruct((CB // 2, BS, BS), jnp.float32),
            in_specs=[pl.BlockSpec(memory_space=pltpu.SMEM)] * 3
            + [pl.BlockSpec(memory_space=pl.ANY)] * 2,
            out_specs=pl.BlockSpec(memory_space=pltpu.VMEM),
            scratch_shapes=[
                *[pltpu.VMEM((CAP + 1, BS, BS), jnp.bfloat16)] * STEPS,
                *[pltpu.VMEM((CAP, BS, BS), jnp.bfloat16)] * STEPS,
                pltpu.VMEM((2, (items + CHUNKS) * LANE, BS, BS), jnp.bfloat16),
                pltpu.VMEM((CB, BS, BS), jnp.float32),
                pltpu.VMEM((CB // 2, BS, BS), jnp.float32),
                dma((4,)),
                dma((2, items)),
                dma((2, items)),
                dma((items,)),
                dma((items,)),
                dma((CAP // LEFT,)),
                dma((2,)),
                dma((2, CHUNKS)),
                dma((STEPS - 1, CAP // 4)),
                dma((STEPS - 1,)),
                dma((2, CHUNKS, NY - 1)),
                dma((CB // 2,)),
                dma((CB // 2,)),
            ],
            compiler_params=pltpu.CompilerParams(
                collective_id=0, has_side_effects=True, vmem_limit_bytes=60 * 2**20
            ),
            name="cannon_window",
        )(
            left_picks.reshape(-1),
            right_picks.reshape(-1),
            live_count.reshape(-1),
            left_panels[0, 0, 0],
            right_panels[0, 0, 0],
        )
        return summed[None, None]

    placed = (
        P("row", "col", "layer", None, None, None),
        P("row", "col", "layer", None, None, None),
        P("row", "col", "layer", None, None, None),
        P("row", "col", "layer", None, None, None),
        P("row", "col", "layer", None, None),
    )
    return jax.shard_map(
        local,
        mesh=mesh,
        in_specs=placed,
        out_specs=P("row", "col", "layer", None, None),
        check_vma=False,
    )
```

```python
import functools

import jax
import jax.numpy as jnp
from jax import lax
from jax.experimental import pallas as pl
from jax.experimental.pallas import tpu as pltpu
from jax.sharding import PartitionSpec as P

MESH = pl.DeviceIdType.MESH

STEPS = 4
NY = 4
BS = 128
CAP = 32
CB = 16
Q = 4
CHUNKS = 3
LANE = 4
LEFT = 2
LEAD = 8


def kernel(
    nx, nc,
    lp_hbm, rp_hbm, live_hbm, left_hbm, right_hbm, out_ref, partner,
    lp_ref, rp_ref, live_ref, left0, left1, left2, left3, right0, right1, right2, right3, lane, totals,
    own_sem, list_sem, lane_send, lane_recv, left_send, left_recv, wrap_send,
    seed_send, seed_recv, near_send, right_recv, spread_send, sum_send, sum_recv,
):
    hops = nc
    items = hops * CHUNKS
    lag = CAP // LEFT
    lefts_at, rights_at = (left0, left1, left2, left3), (right0, right1, right2, right3)
    row = lax.axis_index("row")
    c = lax.axis_index("col")
    l = lax.axis_index("layer")
    x = row // (2 * NY)
    h = (row // NY) % 2
    y = row % NY

    def at(px, ph, py, pc, pll):
        return (px * (2 * NY) + ph * NY + py, pc, pll)

    def ring(px):
        return lax.rem(px + nx, nx)

    first, last = c == 0, c == nc - 1
    up_c = jnp.where(last, 0, c + 1)
    down_c = jnp.where(first, nc - 1, c - 1)
    up_h = jnp.where(last, 1 - h, h)
    down_h = jnp.where(first, 1 - h, h)
    up_next = at(ring(x - jnp.where(last & (h == 0), 1, 0)), up_h, y, up_c, l)
    up_prev = at(ring(x + jnp.where(first & (h == 1), 1, 0)), down_h, y, down_c, l)
    down_next = at(ring(x - jnp.where(first & (h == 0), 1, 0)), down_h, y, down_c, l)
    down_prev = at(ring(x + jnp.where(last & (h == 1), 1, 0)), up_h, y, up_c, l)
    nexts = (up_next, down_next)

    def in_group(py):
        return at(x, h, py, c, l)

    def on_col(pc):
        return at(x, h, y, pc, l)

    sibling = at(x, h, y, c, 1 - l)

    own_left = pltpu.make_async_copy(left_hbm, left0.at[pl.ds(0, CAP)], own_sem.at[0])
    own_right = pltpu.make_async_copy(right_hbm, right0, own_sem.at[1])
    own_left.start()
    own_right.start()
    lists = [
        pltpu.make_async_copy(src, dst, list_sem.at[i])
        for i, (src, dst) in enumerate(((lp_hbm, lp_ref), (rp_hbm, rp_ref), (live_hbm, live_ref)))
    ]
    for copy in lists:
        copy.start()

    def own_lane(d):
        return pltpu.make_async_copy(
            right_hbm.at[pl.ds(d * CHUNKS * LANE, CHUNKS * LANE)],
            lane.at[d, pl.ds(0, CHUNKS * LANE)],
            own_sem.at[2 + d],
        )

    @pl.when(y < NY - 1)
    def _():
        own_lane(0).start()
        own_lane(1).start()

    for panel in lefts_at:
        panel[CAP] = jnp.zeros((BS, BS), panel.dtype)

    barrier = pltpu.get_barrier_semaphore()
    for who in (up_prev, down_prev, sibling):
        pl.semaphore_signal(barrier, inc=1, device_id=who, device_id_type=MESH)
    for k in range(1, NY):
        pl.semaphore_signal(
            barrier, inc=1, device_id=in_group(lax.rem(y + k, NY)), device_id_type=MESH
        )

    @pl.when(c < nc - 1)
    def _():
        pl.semaphore_signal(barrier, inc=1, device_id=on_col(c + 1), device_id_type=MESH)

    @pl.when(last)
    def _():
        for k in range(STEPS - 1):
            pl.semaphore_signal(barrier, inc=1, device_id=on_col(k), device_id_type=MESH)

    greeted = 3 + (NY - 1) + jnp.where(c > 0, 1, 0) + jnp.where(c < STEPS - 1, 1, 0)
    pl.semaphore_wait(barrier, greeted)

    spare = 2 * CHUNKS * LANE

    def seed(d, who):
        return pltpu.make_async_remote_copy(
            src_ref=right_hbm.at[pl.ds(spare + d * LANE, LANE)],
            dst_ref=lane.at[d, pl.ds(who * LANE, LANE)],
            send_sem=seed_send.at[d],
            recv_sem=seed_recv.at[d, who],
            device_id=in_group(NY - 1),
            device_id_type=MESH,
        )

    @pl.when(y < NY - 1)
    def _():
        seed(0, y).start()
        seed(1, y).start()
        own_lane(0).wait()
        own_lane(1).wait()

    own_left.wait()
    own_right.wait()
    for copy in lists:
        copy.wait()

    def lane_copy(d, it):
        return pltpu.make_async_remote_copy(
            src_ref=lane.at[d, pl.ds(it * LANE, LANE)],
            dst_ref=lane.at[d, pl.ds((it + CHUNKS) * LANE, LANE)],
            send_sem=lane_send.at[d, it],
            recv_sem=lane_recv.at[d, it],
            device_id=nexts[d],
            device_id_type=MESH,
        )

    def left_copy(n, step=1):
        block = pl.ds(lax.rem(n, lag) * LEFT, LEFT)
        return pltpu.make_async_remote_copy(
            src_ref=lefts_at[step - 1].at[block],
            dst_ref=lefts_at[step].at[block],
            send_sem=left_send.at[n],
            recv_sem=left_recv.at[n],
            device_id=on_col(jnp.maximum(c - 1, 0)),
            device_id_type=MESH,
        )

    def wrap_copy(n, step=1):
        block = pl.ds(lax.rem(n, lag) * LEFT, LEFT)
        return pltpu.make_async_remote_copy(
            src_ref=left0.at[block],
            dst_ref=lefts_at[step].at[block],
            send_sem=wrap_send.at[lax.rem(n, lag)],
            recv_sem=left_recv.at[n],
            device_id=on_col(nc - 1),
            device_id_type=MESH,
        )

    def left_move(n):
        @pl.when(n >= lag)
        def _():
            left_copy(n - lag).wait_recv()

        for step in range(1, STEPS):

            @pl.when(n // lag == step - 1)
            def _():
                @pl.when(c > 0)
                def _():
                    left_copy(n, step).start()

                @pl.when(c == step - 1)
                def _():
                    wrap_copy(n, step).start()

    def left_run(start, stop):
        lax.fori_loop(start, stop, lambda n, _: (left_move(n), 0)[1], 0)

    near = 4
    near_copies = CAP // near

    def near_copy(s, k):
        return pltpu.make_async_remote_copy(
            src_ref=right0.at[pl.ds(k * near, near)],
            dst_ref=rights_at[s].at[pl.ds(k * near, near)],
            send_sem=near_send.at[s - 1, k],
            recv_sem=right_recv.at[s - 1],
            device_id=in_group(jnp.maximum(y - s, 0)),
            device_id_type=MESH,
        )

    def pair_sum(j, s):
        lefts, rights = [], []
        for q in range(Q):
            used = q < live_ref[s, j]
            lefts.append(lefts_at[s][jnp.where(used, lp_ref[s, q, j], CAP)])
            rights.append(rights_at[s][rp_ref[s, q, j]])
        return jnp.dot(
            jnp.concatenate(lefts, axis=1),
            jnp.concatenate(rights, axis=0),
            preferred_element_type=jnp.float32,
        )

    def step(it, _):
        for d in range(2):

            @pl.when(it >= CHUNKS)
            def _():
                lane_copy(d, it - CHUNKS).wait_recv()

            @pl.when((it < CHUNKS) & (y == NY - 1))
            def _():
                seed(d, it).wait_recv()

            lane_copy(d, it).start()

        @pl.when(lax.rem(it, 2) == 1)
        def _():
            left_move(lead + it // 2)

        @pl.when((it >= CHUNKS) & (it < CHUNKS + near_copies))
        def _():
            for s in range(1, STEPS):

                @pl.when(y >= s)
                def _():
                    near_copy(s, it - CHUNKS).start()

        @pl.when(lax.rem(it, CHUNKS) == 2)
        def _():
            j = it // CHUNKS
            totals[j] = pair_sum(j, 0)

        return 0

    lead = jnp.where(y == NY - 1, LEAD, 0)
    left_run(0, lead)
    lax.fori_loop(0, items, step, 0)

    def arrived(ch):
        return jnp.where(y < NY - 1, y, ch)

    def spread_copy(d, ch, s, to):
        block = jnp.where(y < NY - 1, (d * CHUNKS + ch) * LANE, spare + d * LANE)
        return pltpu.make_async_remote_copy(
            src_ref=lane.at[d, pl.ds((items + ch) * LANE, LANE)],
            dst_ref=rights_at[s].at[pl.ds(block, LANE)],
            send_sem=spread_send.at[d, ch, to - 1],
            recv_sem=right_recv.at[s - 1],
            device_id=in_group(to),
            device_id_type=MESH,
        )

    def spread_here(d, ch):
        return pltpu.make_async_copy(
            lane.at[d, pl.ds((items + ch) * LANE, LANE)],
            rights_at[ch + 1].at[pl.ds(spare + d * LANE, LANE)],
            right_recv.at[ch],
        )

    def each_spread(d, ch, act):
        for to in range(1, NY):
            for src in range(to):

                @pl.when((arrived(ch) == src) & (to != y))
                def _():
                    act(spread_copy(d, ch, NY + src - to, to))

    begun = lead + items // 2
    left_run(begun, begun + 4)
    for ch in range(CHUNKS):
        for d in range(2):
            lane_copy(d, items - CHUNKS + ch).wait_recv()
            each_spread(d, ch, lambda copy: copy.start())

            @pl.when(y == NY - 1)
            def _():
                spread_here(d, ch).start()

        left_run(begun + 4 + 2 * ch, begun + 6 + 2 * ch)
    left_run(begun + 10, items)

    def right_wait(s):
        pltpu.make_async_copy(rights_at[s], rights_at[s], right_recv.at[s - 1]).wait()

    def lanes_gone(it, _):
        for d in range(2):
            lane_copy(d, it).wait_send()

        @pl.when((c > 0) & (it < items - lag))
        def _():
            left_copy(it).wait_send()

        @pl.when(it // lag == c)
        def _():
            wrap_copy(it).wait_send()

        return 0

    lax.fori_loop(0, items, lanes_gone, 0)

    @pl.when(y < NY - 1)
    def _():
        seed(0, y).wait_send()
        seed(1, y).wait_send()

    for s in range(1, STEPS):

        @pl.when(y >= s)
        def _():
            lax.fori_loop(0, near_copies, lambda k, _: (near_copy(s, k).wait_send(), 0)[1], 0)

    right_wait(1)
    right_wait(2)

    def middle(j, _):
        totals[j] = totals[j] + (pair_sum(j, 1) + pair_sum(j, 2))
        return 0

    lax.fori_loop(0, CB, middle, 0)
    right_wait(3)
    for ch in range(CHUNKS):
        for d in range(2):
            each_spread(d, ch, lambda copy: copy.wait_send())

    lax.fori_loop(items - lag, items, lambda n, _: (left_copy(n).wait_recv(), 0)[1], 0)

    half = CB // 2

    def rest(j):
        return totals[j] + pair_sum(j, 3)

    def sum_copy(i):
        return pltpu.make_async_remote_copy(
            src_ref=totals.at[(1 - l) * half + i],
            dst_ref=partner.at[i],
            send_sem=sum_send.at[i],
            recv_sem=sum_recv.at[i],
            device_id=sibling,
            device_id_type=MESH,
        )

    def theirs(i, _):
        j = (1 - l) * half + i
        totals[j] = rest(j)
        sum_copy(i).start()
        return 0

    def ours(i, _):
        out_ref[i] = rest(l * half + i)
        return 0

    lax.fori_loop(0, half, theirs, 0)
    lax.fori_loop(0, half, ours, 0)

    def finish(i, _):
        sum_copy(i).wait_recv()
        sum_copy(i).wait_send()
        return 0

    @pl.when(c > 0)
    def _():
        lax.fori_loop(items - lag, items, lambda n, _: (left_copy(n).wait_send(), 0)[1], 0)

    lax.fori_loop(0, half, finish, 0)


def solution(mesh):
    nx = mesh.shape["row"] // (2 * NY)
    nc = mesh.shape["col"]
    items = nc * CHUNKS
    dma = pltpu.SemaphoreType.DMA

    def local(left_panels, right_panels, left_picks, right_picks, live_count):
        own, partner = pl.pallas_call(
            functools.partial(kernel, nx, nc),
            out_shape=[jax.ShapeDtypeStruct((CB // 2, BS, BS), jnp.float32)] * 2,
            in_specs=[pl.BlockSpec(memory_space=pltpu.HBM)] * 5,
            out_specs=[pl.BlockSpec(memory_space=pltpu.VMEM)] * 2,
            scratch_shapes=[
                pltpu.SMEM((STEPS, Q, CB), jnp.int32),
                pltpu.SMEM((STEPS, Q, CB), jnp.int32),
                pltpu.SMEM((STEPS, CB), jnp.int32),
                *[pltpu.VMEM((CAP + 1, BS, BS), jnp.bfloat16)] * STEPS,
                *[pltpu.VMEM((CAP, BS, BS), jnp.bfloat16)] * STEPS,
                pltpu.VMEM((2, (items + CHUNKS) * LANE, BS, BS), jnp.bfloat16),
                pltpu.VMEM((CB, BS, BS), jnp.float32),
                dma((4,)),
                dma((3,)),
                dma((2, items)),
                dma((2, items)),
                dma((items,)),
                dma((items,)),
                dma((CAP // LEFT,)),
                dma((2,)),
                dma((2, CHUNKS)),
                dma((STEPS - 1, CAP // 4)),
                dma((STEPS - 1,)),
                dma((2, CHUNKS, NY - 1)),
                dma((CB // 2,)),
                dma((CB // 2,)),
            ],
            compiler_params=pltpu.CompilerParams(
                collective_id=0, has_side_effects=True, vmem_limit_bytes=60 * 2**20
            ),
            name="cannon_window",
        )(
            jnp.swapaxes(left_picks[0, 0, 0], 1, 2),
            jnp.swapaxes(right_picks[0, 0, 0], 1, 2),
            live_count[0, 0, 0],
            left_panels[0, 0, 0],
            right_panels[0, 0, 0],
        )
        return (own + partner)[None, None]

    placed = (
        P("row", "col", "layer", None, None, None),
        P("row", "col", "layer", None, None, None),
        P("row", "col", "layer", None, None, None),
        P("row", "col", "layer", None, None, None),
        P("row", "col", "layer", None, None),
    )
    return jax.shard_map(
        local,
        mesh=mesh,
        in_specs=placed,
        out_specs=P("row", "col", "layer", None, None),
        check_vma=False,
    )
```

```python
import functools

import jax
import jax.numpy as jnp
from jax import lax
from jax.experimental import pallas as pl
from jax.experimental.pallas import tpu as pltpu
from jax.sharding import PartitionSpec as P

MESH = pl.DeviceIdType.MESH

STEPS = 4
NY = 4
BS = 128
CAP = 32
CB = 16
Q = 4
CHUNKS = 3
LANE = 4
LEFT = 2
UNROLL = 4
AHEAD = 16
LEAD = 8


def kernel(
    nx, nc,
    lp_hbm, rp_hbm, live_hbm, left_hbm, right_hbm, out_ref, partner,
    lp_ref, rp_ref, live_ref, left0, left1, left2, left3, right0, right1, right2, right3, lane, totals,
    own_sem, list_sem, lane_send, lane_recv, left_send, left_recv, wrap_send,
    seed_send, seed_recv, near_send, right_recv, spread_send, sum_send, sum_recv,
    down_ready, wrap_ready,
):
    hops = nc
    items = hops * CHUNKS
    lag = CAP // LEFT
    lefts_at, rights_at = (left0, left1, left2, left3), (right0, right1, right2, right3)
    row = lax.axis_index("row")
    c = lax.axis_index("col")
    l = lax.axis_index("layer")
    x = row // (2 * NY)
    h = (row // NY) % 2
    y = row % NY

    def at(px, ph, py, pc, pll):
        return (px * (2 * NY) + ph * NY + py, pc, pll)

    def ring(px):
        return lax.rem(px + nx, nx)

    first, last = c == 0, c == nc - 1
    up_c = jnp.where(last, 0, c + 1)
    down_c = jnp.where(first, nc - 1, c - 1)
    up_h = jnp.where(last, 1 - h, h)
    down_h = jnp.where(first, 1 - h, h)
    up_next = at(ring(x - jnp.where(last & (h == 0), 1, 0)), up_h, y, up_c, l)
    up_prev = at(ring(x + jnp.where(first & (h == 1), 1, 0)), down_h, y, down_c, l)
    down_next = at(ring(x - jnp.where(first & (h == 0), 1, 0)), down_h, y, down_c, l)
    down_prev = at(ring(x + jnp.where(last & (h == 1), 1, 0)), up_h, y, up_c, l)
    nexts = (up_next, down_next)

    def in_group(py):
        return at(x, h, py, c, l)

    def on_col(pc):
        return at(x, h, y, pc, l)

    sibling = at(x, h, y, c, 1 - l)

    barrier = pltpu.get_barrier_semaphore()
    def greet(who):
        pl.semaphore_signal(barrier, inc=1, device_id=who, device_id_type=MESH)

    greet(up_prev)
    greet(sibling)
    for k in range(1, NY):
        greet(in_group(lax.rem(y + k, NY)))

    @pl.when(c < nc - 1)
    def _():
        greet(down_prev)
        greet(on_col(c + 1))

    @pl.when(first)
    def _():
        greet(down_next)

    @pl.when(c < STEPS - 1)
    def _():
        greet(on_col(nc - 1))

    greeted = 2 + (NY - 1) + jnp.where(c > 0, 2, 0) + jnp.where(last, STEPS, 0)

    own_left = pltpu.make_async_copy(left_hbm, left0.at[pl.ds(0, CAP)], own_sem.at[0])
    own_right = pltpu.make_async_copy(right_hbm, right0, own_sem.at[1])
    own_left.start()
    own_right.start()
    lists = [
        pltpu.make_async_copy(src, dst, list_sem.at[i])
        for i, (src, dst) in enumerate(((lp_hbm, lp_ref), (rp_hbm, rp_ref), (live_hbm, live_ref)))
    ]
    for copy in lists:
        copy.start()

    for panel in lefts_at:
        panel[CAP] = jnp.zeros((BS, BS), panel.dtype)

    pl.semaphore_wait(barrier, greeted)

    @pl.when(last)
    def _():
        pl.semaphore_signal(down_ready, inc=1, device_id=down_prev, device_id_type=MESH)
        for k in range(STEPS - 1):
            pl.semaphore_signal(wrap_ready, inc=1, device_id=on_col(k), device_id_type=MESH)

    spare = 2 * CHUNKS * LANE

    def seed(d, who):
        return pltpu.make_async_remote_copy(
            src_ref=right_hbm.at[pl.ds(spare + d * LANE, LANE)],
            dst_ref=lane.at[d, pl.ds(who * LANE, LANE)],
            send_sem=seed_send.at[d],
            recv_sem=seed_recv.at[d, who],
            device_id=in_group(NY - 1),
            device_id_type=MESH,
        )

    @pl.when(y < NY - 1)
    def _():
        seed(0, y).start()
        seed(1, y).start()


    def lane_copy(d, it, src=None):
        return pltpu.make_async_remote_copy(
            src_ref=lane.at[d, pl.ds(it * LANE, LANE)] if src is None else src,
            dst_ref=lane.at[d, pl.ds((it + CHUNKS) * LANE, LANE)],
            send_sem=lane_send.at[d, it],
            recv_sem=lane_recv.at[d, it],
            device_id=nexts[d],
            device_id_type=MESH,
        )

    def left_copy(n, step=1):
        block = pl.ds(lax.rem(n, lag) * LEFT, LEFT)
        return pltpu.make_async_remote_copy(
            src_ref=(left_hbm if step == 1 else lefts_at[step - 1]).at[block],
            dst_ref=lefts_at[step].at[block],
            send_sem=left_send.at[n],
            recv_sem=left_recv.at[n],
            device_id=on_col(jnp.maximum(c - 1, 0)),
            device_id_type=MESH,
        )

    def wrap_copy(n, step=1):
        block = pl.ds(lax.rem(n, lag) * LEFT, LEFT)
        return pltpu.make_async_remote_copy(
            src_ref=left_hbm.at[block],
            dst_ref=lefts_at[step].at[block],
            send_sem=wrap_send.at[lax.rem(n, lag)],
            recv_sem=left_recv.at[n],
            device_id=on_col(nc - 1),
            device_id_type=MESH,
        )

    def left_move(n):
        @pl.when(n >= lag)
        def _():
            left_copy(n - lag).wait_recv()

        for step in range(1, STEPS):

            @pl.when(n // lag == step - 1)
            def _():
                @pl.when(c > 0)
                def _():
                    left_copy(n, step).start()

    def wrap_move(n):
        @pl.when(n == c * lag)
        def _():
            pl.semaphore_wait(wrap_ready, 1)

        for step in range(1, STEPS):

            @pl.when((n // lag == step - 1) & (c == step - 1))
            def _():
                wrap_copy(n, step).start()

    def wrap_run(start, stop):
        @pl.when(c < STEPS - 1)
        def _():
            lax.fori_loop(start, stop, lambda n, _: (wrap_move(n), 0)[1], 0)

    def left_run(start, stop):
        lax.fori_loop(start, stop, lambda n, _: (left_move(n), 0)[1], 0)

    near = 4
    near_copies = CAP // near

    def near_copy(s, k):
        return pltpu.make_async_remote_copy(
            src_ref=right_hbm.at[pl.ds(k * near, near)],
            dst_ref=rights_at[s].at[pl.ds(k * near, near)],
            send_sem=near_send.at[s - 1, k],
            recv_sem=right_recv.at[s - 1],
            device_id=in_group(jnp.maximum(y - s, 0)),
            device_id_type=MESH,
        )

    def pair_sum(j, s):
        lefts, rights = [], []
        for q in range(Q):
            used = q < live_ref[s, j]
            lefts.append(lefts_at[s][jnp.where(used, lp_ref[s, q, j], CAP)])
            rights.append(rights_at[s][rp_ref[s, q, j]])
        return jnp.dot(
            jnp.concatenate(lefts, axis=1),
            jnp.concatenate(rights, axis=0),
            preferred_element_type=jnp.float32,
        )

    def lane_move(d, k):
        @pl.when(k >= CHUNKS)
        def _():
            lane_copy(d, k - CHUNKS).wait_recv()

        @pl.when((k < CHUNKS) & (y == NY - 1))
        def _():
            seed(d, k).wait_recv()

        @pl.when((k < CHUNKS) & (y < NY - 1))
        def _():
            lane_copy(d, k, right_hbm.at[pl.ds((d * CHUNKS + k) * LANE, LANE)]).start()

        @pl.when((k >= CHUNKS) | (y == NY - 1))
        def _():
            lane_copy(d, k).start()

    ahead = jnp.where((h == 0) & (c > 0) & (y < NY - 1), jnp.maximum(AHEAD - c, 0) // 4, 0)

    lead = jnp.where(y == NY - 1, LEAD, 0)
    def step(it, _):
        up = it - ahead

        @pl.when(up >= CHUNKS)
        def _():
            lane_move(0, up)

        @pl.when((it == 0) & first)
        def _():
            pl.semaphore_wait(down_ready, 1)

        @pl.when(it < items)
        def _():
            lane_move(1, it)

        @pl.when((lax.rem(it, 2) == 1) & (it < items))
        def _():
            left_move(lead + it // 2)

            @pl.when(c < STEPS - 1)
            def _():
                wrap_move(it // 2)

        @pl.when((it >= CHUNKS) & (it < CHUNKS + near_copies))
        def _():
            for s in range(1, STEPS):

                @pl.when(y >= s)
                def _():
                    near_copy(s, it - CHUNKS).start()

        @pl.when((lax.rem(it, CHUNKS) == 2) & (it < items))
        def _():
            j = it // CHUNKS
            totals[j] = pair_sum(j, 0)

        return 0

    left_run(0, lead)
    for k in range(CHUNKS):
        lane_move(0, k)
    own_left.wait()
    own_right.wait()
    for copy in lists:
        copy.wait()
    lax.fori_loop(0, items + ahead, step, 0)

    def arrived(ch):
        return jnp.where(y < NY - 1, y, ch)

    def spread_copy(d, ch, s, to):
        block = jnp.where(y < NY - 1, (d * CHUNKS + ch) * LANE, spare + d * LANE)
        return pltpu.make_async_remote_copy(
            src_ref=lane.at[d, pl.ds((items + ch) * LANE, LANE)],
            dst_ref=rights_at[s].at[pl.ds(block, LANE)],
            send_sem=spread_send.at[d, ch, to - 1],
            recv_sem=right_recv.at[s - 1],
            device_id=in_group(to),
            device_id_type=MESH,
        )

    def spread_here(d, ch):
        return pltpu.make_async_copy(
            lane.at[d, pl.ds((items + ch) * LANE, LANE)],
            rights_at[ch + 1].at[pl.ds(spare + d * LANE, LANE)],
            right_recv.at[ch],
        )

    def each_spread(d, ch, act):
        for to in range(1, NY):
            for src in range(to):

                @pl.when((arrived(ch) == src) & (to != y))
                def _():
                    act(spread_copy(d, ch, NY + src - to, to))

    begun = lead + items // 2
    wrap_run(items // 2, items)
    left_run(begun, begun + 4)
    for ch in range(CHUNKS):
        for d in range(2):
            lane_copy(d, items - CHUNKS + ch).wait_recv()
            each_spread(d, ch, lambda copy: copy.start())

            @pl.when(y == NY - 1)
            def _():
                spread_here(d, ch).start()

        left_run(begun + 4 + 2 * ch, begun + 6 + 2 * ch)
    left_run(begun + 10, items)

    def right_wait(s):
        pltpu.make_async_copy(rights_at[s], rights_at[s], right_recv.at[s - 1]).wait()

    def lanes_gone(it, _):
        for d in range(2):
            lane_copy(d, it).wait_send()

        @pl.when((c > 0) & (it < items - lag))
        def _():
            left_copy(it).wait_send()

        return 0

    lax.fori_loop(0, items, lanes_gone, 0)

    @pl.when(y < NY - 1)
    def _():
        seed(0, y).wait_send()
        seed(1, y).wait_send()

    for s in range(1, STEPS):

        @pl.when(y >= s)
        def _():
            lax.fori_loop(0, near_copies, lambda k, _: (near_copy(s, k).wait_send(), 0)[1], 0)

    right_wait(1)
    right_wait(2)

    def middle(j, _):
        totals[j] = totals[j] + (pair_sum(j, 1) + pair_sum(j, 2))
        return 0

    lax.fori_loop(0, CB, middle, 0, unroll=UNROLL)
    right_wait(3)
    for ch in range(CHUNKS):
        for d in range(2):
            each_spread(d, ch, lambda copy: copy.wait_send())

    lax.fori_loop(items - lag, items, lambda n, _: (left_copy(n).wait_recv(), 0)[1], 0)

    half = CB // 2

    def rest(j):
        return totals[j] + pair_sum(j, 3)

    def sum_copy(i):
        return pltpu.make_async_remote_copy(
            src_ref=totals.at[(1 - l) * half + i],
            dst_ref=partner.at[i],
            send_sem=sum_send.at[i],
            recv_sem=sum_recv.at[i],
            device_id=sibling,
            device_id_type=MESH,
        )

    def theirs(i, _):
        j = (1 - l) * half + i
        totals[j] = rest(j)
        sum_copy(i).start()
        return 0

    def ours(i, _):
        out_ref[i] = rest(l * half + i)
        return 0

    lax.fori_loop(0, half, theirs, 0, unroll=UNROLL)
    lax.fori_loop(0, half, ours, 0, unroll=UNROLL)

    def finish(i, _):
        sum_copy(i).wait_recv()
        sum_copy(i).wait_send()
        return 0

    @pl.when(c > 0)
    def _():
        lax.fori_loop(items - lag, items, lambda n, _: (left_copy(n).wait_send(), 0)[1], 0)

    @pl.when(c < STEPS - 1)
    def _():
        lax.fori_loop(0, lag, lambda n, _: (wrap_copy(n).wait_send(), 0)[1], 0)

    lax.fori_loop(0, half, finish, 0)


def solution(mesh):
    nx = mesh.shape["row"] // (2 * NY)
    nc = mesh.shape["col"]
    items = nc * CHUNKS
    dma = pltpu.SemaphoreType.DMA

    def local(left_panels, right_panels, left_picks, right_picks, live_count):
        own, partner = pl.pallas_call(
            functools.partial(kernel, nx, nc),
            out_shape=[jax.ShapeDtypeStruct((CB // 2, BS, BS), jnp.float32)] * 2,
            in_specs=[pl.BlockSpec(memory_space=pltpu.HBM)] * 5,
            out_specs=[pl.BlockSpec(memory_space=pltpu.VMEM)] * 2,
            scratch_shapes=[
                pltpu.SMEM((STEPS, Q, CB), jnp.int32),
                pltpu.SMEM((STEPS, Q, CB), jnp.int32),
                pltpu.SMEM((STEPS, CB), jnp.int32),
                *[pltpu.VMEM((CAP + 1, BS, BS), jnp.bfloat16)] * STEPS,
                *[pltpu.VMEM((CAP, BS, BS), jnp.bfloat16)] * STEPS,
                pltpu.VMEM((2, (items + CHUNKS) * LANE, BS, BS), jnp.bfloat16),
                pltpu.VMEM((CB, BS, BS), jnp.float32),
                dma((2,)),
                dma((3,)),
                dma((2, items)),
                dma((2, items)),
                dma((items,)),
                dma((items,)),
                dma((CAP // LEFT,)),
                dma((2,)),
                dma((2, CHUNKS)),
                dma((STEPS - 1, CAP // 4)),
                dma((STEPS - 1,)),
                dma((2, CHUNKS, NY - 1)),
                dma((CB // 2,)),
                dma((CB // 2,)),
                pltpu.SemaphoreType.REGULAR,
                pltpu.SemaphoreType.REGULAR,
            ],
            compiler_params=pltpu.CompilerParams(
                collective_id=0, has_side_effects=True, vmem_limit_bytes=60 * 2**20
            ),
            name="cannon_window",
        )(
            jnp.swapaxes(left_picks[0, 0, 0], 1, 2),
            jnp.swapaxes(right_picks[0, 0, 0], 1, 2),
            live_count[0, 0, 0],
            left_panels[0, 0, 0],
            right_panels[0, 0, 0],
        )
        return (own + partner)[None, None]

    placed = (
        P("row", "col", "layer", None, None, None),
        P("row", "col", "layer", None, None, None),
        P("row", "col", "layer", None, None, None),
        P("row", "col", "layer", None, None, None),
        P("row", "col", "layer", None, None),
    )
    return jax.shard_map(
        local,
        mesh=mesh,
        in_specs=placed,
        out_specs=P("row", "col", "layer", None, None),
        check_vma=False,
    )
```
